32 devices in a mesh: seq: 8 (over y, x, core), head: 4 (over z).
Axes of the slice: x: 2, y: 2, z: 4, core: 2. Of those that a mesh axis runs over, the one named last changes fastest.
Arguments:
- queries: bfloat16 [4096, 3072], P(('seq', 'head')), may hold values from -8 to 8
- key_vectors: bfloat16 [4096, 3072], P(('seq', 'head')), may hold values from -8 to 8
- value_vectors: bfloat16 [4096, 3072], P(('seq', 'head')), may hold values from -6 to 6
- block_mask: int32 [24, 32, 32], P('head'), may hold values from 0 to 1, as said below
- layout: int32 [32], replicated, may hold values from 0 to 31, as said below
Outputs:
- attended: bfloat16 [4096, 3072], P(('seq', 'head'))
The draws below stay inside these ranges and needn't reach their ends.
Inputs may be any that keep to these rules, and one draw needn't show every extreme that they name: block_mask[h, c, c] = 1 for every head h and block c. `layout`: a permutation of the block numbers.
All inputs are finite; a program needn't handle non-finite values.
Results may differ from the reference program's by a relative error of at most 0.0035.
Values may be sent and summed in bfloat16 or wider, within the bound.
No kernel may reach another device: no remote copies, remote signals or barrier semaphores. Data moves between devices by JAX's collectives and lax.ppermute only.
A program may use at most 128 MiB of HBM per device.

```python
import math
import jax
import jax.numpy as jnp
from jax import lax

HEADS = 24
HEAD_DIM = 128
BLOCK = 128
D = 3072
TOKENS = 4096
NBLOCKS = 32


def base_rows(key):
    values = jnp.clip(2.0 * jax.random.normal(key, (TOKENS, D), jnp.float32), -8.0, 8.0)
    return values


def draw_queries(key, part):
    values = base_rows(jax.random.fold_in(key, 1))
    return values.astype(jnp.bfloat16)


def draw_key_vectors(key, part):
    values = base_rows(jax.random.fold_in(key, 2))
    return values.astype(jnp.bfloat16)


def mask_and_layout(key):
    layout = jax.random.permutation(jax.random.fold_in(key, 3), NBLOCKS).astype(jnp.int32)
    position = jnp.arange(NBLOCKS, dtype=jnp.int32)
    limit = 50 + 900 * position * position // ((NBLOCKS - 1) * (NBLOCKS - 1))
    coins = jax.random.randint(jax.random.fold_in(key, 5), (HEADS, NBLOCKS, NBLOCKS), 0, 1000, dtype=jnp.int32)
    stored_rows = (coins < limit[None, :, None]).astype(jnp.int32)
    mask = jnp.zeros((HEADS, NBLOCKS, NBLOCKS), jnp.int32).at[:, layout, :].set(stored_rows)
    diagonal = (position[:, None] == position[None, :]).astype(jnp.int32)
    return (jnp.maximum(mask, diagonal[None, :, :]), layout)


def draw_block_mask(key, part):
    mask, layout = mask_and_layout(key)
    return mask


def draw_layout(key, part):
    mask, layout = mask_and_layout(key)
    return layout


def shard_levels(stream_key, dims, shards, low, largest):
    factor_of, own = 1.0, jax.random.fold_in(stream_key, 6)
    for axis_at, shards_of in shards:
        heights = jnp.exp(jax.random.uniform(jax.random.fold_in(own, axis_at), (shards_of,), jnp.float32, low / len(shards), largest / len(shards)))
        factor_of = factor_of * jnp.repeat(heights, dims[axis_at] // shards_of).reshape([-1 if axis == axis_at else 1 for axis in range(len(dims))])
    return factor_of


def noise(stream_key, shape, spread, most, cuts=(), held_as=jnp.bfloat16):
    values = spread * jax.random.normal(stream_key, shape, jnp.float32)
    if cuts:
        values = values * shard_levels(stream_key, shape, cuts, -0.22, 0.18)
    return jnp.clip(values, -most, most).astype(held_as)


def setup_inputs(seed: int = 0) -> dict:
    arg_keys = jax.random.split(jax.random.key(seed), 6)
    return {
        "queries": draw_queries(jax.random.fold_in(arg_keys[5], 71), 0),
        "key_vectors": draw_key_vectors(jax.random.fold_in(arg_keys[5], 71), 0),
        "value_vectors": noise(arg_keys[2], (TOKENS, D), 1.0, 6.0, ((0, 32),)),
        "block_mask": draw_block_mask(jax.random.fold_in(arg_keys[5], 71), 0),
        "layout": draw_layout(jax.random.fold_in(arg_keys[5], 71), 0),
    }


def stored_mask(block_mask, layout):
    count = layout.shape[0]
    select = (layout[:, None] == jnp.arange(count, dtype=jnp.int32)[None, :]).astype(jnp.float32)
    return jnp.einsum('jc,hce,ke->hjk', select, block_mask.astype(jnp.float32), select, precision=lax.Precision.HIGHEST)

def reference(queries, key_vectors, value_vectors, block_mask, layout):
    tokens = queries.shape[0]
    scale = 1.0 / math.sqrt(HEAD_DIM)
    masks = stored_mask(block_mask, layout)
    group_rows = 2 * BLOCK
    groups = tokens // group_rows

    def split_heads(array):
        return jnp.transpose(array.astype(jnp.float32).reshape(tokens, HEADS, HEAD_DIM), (1, 0, 2))
    query_heads = split_heads(queries)
    key_heads = split_heads(key_vectors)
    value_heads = split_heads(value_vectors)

    def one_head(inputs):
        query_head, key_head, value_head, mask_head = inputs

        def one_group(index):
            rows_q = lax.dynamic_slice_in_dim(query_head, index * group_rows, group_rows, 0)
            mask_rows = lax.dynamic_slice_in_dim(mask_head, index * 2, 2, 0)
            allowed = jnp.repeat(jnp.repeat(mask_rows, BLOCK, axis=0), BLOCK, axis=1) > 0.5
            scores = jnp.dot(rows_q, key_head.T, precision=lax.Precision.HIGHEST) * scale
            scores = jnp.where(allowed, scores, -jnp.inf)
            rowmax = lax.optimization_barrier(jnp.max(scores, axis=1, keepdims=True))
            probs = jnp.where(allowed, jnp.exp(scores - rowmax), jnp.float32(0.0))
            total = lax.optimization_barrier(jnp.sum(probs, axis=1, keepdims=True))
            weights = lax.optimization_barrier(probs.astype(jnp.bfloat16)).astype(jnp.float32)
            summed = jnp.dot(weights, value_head, precision=lax.Precision.HIGHEST)
            return (summed / total).astype(jnp.bfloat16)
        outputs = lax.map(one_group, jnp.arange(groups, dtype=jnp.int32))
        return outputs.reshape(tokens, HEAD_DIM)
    result = lax.map(one_head, (query_heads, key_heads, value_heads, masks))
    return jnp.transpose(result, (1, 0, 2)).reshape(tokens, HEADS * HEAD_DIM)
```

```python
import math

import jax
import jax.numpy as jnp
from jax import lax
from jax.experimental import pallas as pl
from jax.experimental.pallas import tpu as pltpu
from jax.sharding import PartitionSpec as P

HEAD_DIM = 128
BLOCK = 128
EXP2_SCALE = math.log2(math.e) / math.sqrt(HEAD_DIM)
KERNEL_VMEM = 56 * 2**20
SCORE_BYTES = 8 * 2**20


def pack(place, sources, heads_here, first_head, chunk, ways):
    rows = sources[0].shape[0]
    message = jax.ShapeDtypeStruct((chunk, 3, rows, HEAD_DIM), sources[0].dtype)

    def body(place_ref, *refs):
        for way in range(ways):
            for part in range(3):
                block = refs[way * 3 + part][...]
                for head in range(chunk):
                    refs[3 * ways + way][head, part] = block[
                        :, head * HEAD_DIM : (head + 1) * HEAD_DIM
                    ]

    def lanes(way):
        return lambda step, place: (0, ((place[1] ^ way) * heads_here + first_head) // chunk)

    return pl.pallas_call(
        body,
        grid_spec=pltpu.PrefetchScalarGridSpec(
            num_scalar_prefetch=1,
            grid=(1,),
            in_specs=[
                pl.BlockSpec((rows, chunk * HEAD_DIM), lanes(way))
                for way in range(ways)
                for part in range(3)
            ],
            out_specs=[pl.BlockSpec(message.shape, lambda *_: (0, 0, 0, 0))] * ways,
        ),
        out_shape=[message] * ways,
        name="pack",
    )(place, *[source for way in range(ways) for source in sources])


def unpack(place, pieces, rows, width, heads_here, chunk, ways):
    flat = [piece for group in pieces for piece in group]
    count = len(flat)

    def body(place_ref, *refs):
        for index in range(count):
            which, way = divmod(index, ways)
            for head in range(chunk):
                lane = ((place_ref[1] ^ way) * heads_here + which * chunk + head) * HEAD_DIM
                refs[count][:, pl.ds(pl.multiple_of(lane, HEAD_DIM), HEAD_DIM)] = refs[index][head]

    return pl.pallas_call(
        body,
        grid_spec=pltpu.PrefetchScalarGridSpec(
            num_scalar_prefetch=1,
            grid=(1,),
            in_specs=[pl.BlockSpec((chunk, rows, HEAD_DIM), lambda *_: (0, 0, 0))] * count,
            out_specs=pl.BlockSpec((rows, width), lambda *_: (0, 0)),
        ),
        out_shape=jax.ShapeDtypeStruct((rows, width), flat[0].dtype),
        name="unpack",
    )(place, *flat)


def attend(place, layout, key_ids, block_mask, first_head, queries, parts):
    chunk, _, rows, _ = queries[0].shape
    ways = len(queries)
    members = parts[0].shape[0]
    fold = BLOCK // rows
    units = ways // fold
    blocks = len(parts) * members * units
    width = blocks * BLOCK
    group = max(1, min(units, SCORE_BYTES // (4 * BLOCK * width)))

    def body(place_ref, layout_ref, ids_ref, mask_ref, *refs):
        query_refs, part_refs = refs[:ways], refs[ways : ways + len(parts)]
        out_refs, scores = refs[ways + len(parts) : -1], refs[-1]

        for start in range(0, units, group):
            tile = jnp.concatenate(
                [query_refs[way][0, 0] for way in range(start * fold, (start + group) * fold)],
                axis=0,
            )
            mask_rows = [
                layout_ref[
                    (place_ref[0] * ways + (place_ref[1] ^ ((start + at) * fold))) // fold
                ]
                for at in range(group)
            ]
            maxima = [None] * group
            block = 0
            for part in part_refs:
                for member in range(members):
                    keys = part[member, 0, 0].reshape(units * BLOCK, HEAD_DIM)
                    found = lax.dot_general(
                        tile,
                        keys,
                        (((1,), (1,)), ((), ())),
                        preferred_element_type=jnp.float32,
                    )
                    for unit in range(units):
                        column = layout_ref[ids_ref[block]]
                        for at in range(group):
                            allowed = mask_ref[0, mask_rows[at], column] > 0
                            bias = jnp.where(allowed, jnp.float32(0), jnp.float32(-jnp.inf))
                            piece = (
                                found[
                                    at * BLOCK : (at + 1) * BLOCK,
                                    unit * BLOCK : (unit + 1) * BLOCK,
                                ]
                                + bias
                            )
                            scores[
                                at * BLOCK : (at + 1) * BLOCK, block * BLOCK : (block + 1) * BLOCK
                            ] = piece
                            maxima[at] = (
                                piece if maxima[at] is None else jnp.maximum(maxima[at], piece)
                            )
                        block += 1
            for at in range(group):
                shift = jnp.max(maxima[at], axis=1, keepdims=True) * EXP2_SCALE
                total = accum = None
                block = 0
                for part in part_refs:
                    for member in range(members):
                        wide = scores[
                            at * BLOCK : (at + 1) * BLOCK, block * BLOCK : (block + units) * BLOCK
                        ]
                        probs = jnp.exp2(wide * EXP2_SCALE - shift)
                        for unit in range(units):
                            piece = probs[:, unit * BLOCK : (unit + 1) * BLOCK]
                            total = piece if total is None else total + piece
                        values = part[member, 0, 1].reshape(units * BLOCK, HEAD_DIM)
                        product = jnp.dot(
                            probs.astype(jnp.bfloat16), values, preferred_element_type=jnp.float32
                        )
                        accum = product if accum is None else accum + product
                        block += units
                total = jnp.sum(total, axis=1, keepdims=True)
                result = (accum / total).astype(jnp.bfloat16)
                for piece in range(fold):
                    out_refs[(start + at) * fold + piece][0] = result[
                        piece * rows : (piece + 1) * rows
                    ]

    return pl.pallas_call(
        body,
        grid_spec=pltpu.PrefetchScalarGridSpec(
            num_scalar_prefetch=3,
            grid=(chunk,),
            in_specs=[
                pl.BlockSpec(
                    (1, blocks, blocks),
                    lambda head, *_: (first_head + head, 0, 0),
                    memory_space=pltpu.SMEM,
                )
            ]
            + [pl.BlockSpec((1, 1, rows, HEAD_DIM), lambda head, *_: (head, 2, 0, 0))] * ways
            + [
                pl.BlockSpec(
                    (members, 1, 2, ways, rows, HEAD_DIM), lambda head, *_: (0, head, 0, 0, 0, 0)
                )
            ]
            * len(parts),
            out_specs=[pl.BlockSpec((1, rows, HEAD_DIM), lambda head, *_: (head, 0, 0))] * ways,
            scratch_shapes=[pltpu.VMEM((group * BLOCK, width), jnp.float32)],
        ),
        out_shape=[jax.ShapeDtypeStruct((chunk, rows, HEAD_DIM), jnp.bfloat16)] * ways,
        compiler_params=pltpu.CompilerParams(vmem_limit_bytes=KERNEL_VMEM),
        cost_estimate=pl.CostEstimate(
            flops=4 * chunk * ways * rows * width * HEAD_DIM,
            bytes_accessed=4 * chunk * width * HEAD_DIM,
            transcendentals=chunk * ways * rows * width,
        ),
        name="attend",
    )(place, layout, key_ids, block_mask, *queries, *parts)


def gather_parts(shared, seq_count, seq, ways):
    if seq_count != 8:
        whole = lax.all_gather(shared, "seq", axis=0)
        return [whole], jnp.arange(seq_count, dtype=jnp.int32)
    near = [(s, s ^ (4 if s & 1 else 2)) for s in range(8)]
    far = [(s, s ^ (2 if s & 1 else 4)) for s in range(8)]
    core = [(s, s ^ 1) for s in range(8)]
    first = lax.ppermute(shared, "seq", near)
    second = lax.ppermute(shared, "seq", far)
    third = lax.ppermute(first, "seq", far)
    own = [shared, first, second, third]
    other = [lax.ppermute(part, "seq", core) for part in own]
    flip = jnp.where(seq % 2 == 0, 2, 4)
    owners = [seq, seq ^ flip, seq ^ 6 ^ flip, seq ^ 6]
    owners += [seq ^ 1, seq ^ 1 ^ 6 ^ flip, seq ^ 1 ^ flip, seq ^ 7]
    return [part[None] for part in own + other], jnp.stack(owners).astype(jnp.int32)


def per_device(queries, key_vectors, value_vectors, block_mask, layout):
    ways, seq_count = lax.axis_size("head"), lax.axis_size("seq")
    seq, place_z = lax.axis_index("seq"), lax.axis_index("head")
    rows, width = queries.shape
    heads_here = width // HEAD_DIM // ways
    assert BLOCK % rows == 0 and ways & (ways - 1) == 0 and ways * rows % BLOCK == 0
    fold = BLOCK // rows
    chunk = max(1, heads_here // 3)
    place = jnp.stack([seq, place_z]).astype(jnp.int32)

    def swap(array, way):
        return lax.ppermute(array, "head", [(z, z ^ way) for z in range(ways)])

    returned = []
    for first_head in range(0, heads_here, chunk):
        sent = pack(
            place, (key_vectors, value_vectors, queries), heads_here, first_head, chunk, ways
        )
        held = [sent[0]] + [swap(sent[way], way) for way in range(1, ways)]
        shared = jnp.stack([message[:, :2] for message in held], axis=2)
        parts, owners = gather_parts(shared, seq_count, seq, ways)
        others = place_z ^ jnp.arange(0, ways, fold, dtype=jnp.int32)
        key_ids = ((owners[:, None] * ways + others[None, :]) // fold).reshape(-1)
        outs = attend(place, layout, key_ids, block_mask, first_head, held, parts)
        returned.append([outs[0]] + [swap(outs[way], way) for way in range(1, ways)])
    return unpack(place, returned, rows, width, heads_here, chunk, ways)


def solution(mesh):
    placed = (
        P(("seq", "head"), None),
        P(("seq", "head"), None),
        P(("seq", "head"), None),
        P("head", None, None),
        P(),
    )
    return jax.shard_map(
        per_device, mesh=mesh, in_specs=placed, out_specs=P(("seq", "head"), None), check_vma=False
    )
```

```python
import math

import jax
import jax.numpy as jnp
from jax import lax
from jax.experimental import pallas as pl
from jax.experimental.pallas import tpu as pltpu
from jax.sharding import PartitionSpec as P

HEAD_DIM = 128
BLOCK = 128
EXP2_SCALE = math.log2(math.e) / math.sqrt(HEAD_DIM)
KERNEL_VMEM = 32 * 2**20
SCORE_BYTES = 8 * 2**20


def head_lane(place_ref, way, other, turn, shape):
    cores, turns = shape
    core = place_ref[0] ^ other if cores > 1 else 0
    head = ((place_ref[1] ^ way) * cores + core) * turns + turn
    return pl.ds(pl.multiple_of(head * HEAD_DIM, HEAD_DIM), HEAD_DIM)


def in_vmem(body, out_shape, name, place, *operands):
    return pl.pallas_call(
        body,
        in_specs=[pl.BlockSpec(memory_space=pltpu.SMEM)]
        + [pl.BlockSpec(memory_space=pltpu.VMEM)] * len(operands),
        out_specs=jax.tree.map(lambda _: pl.BlockSpec(memory_space=pltpu.VMEM), out_shape),
        out_shape=out_shape,
        name=name,
    )(place, *operands)


def pack_twin(place, sources, parts, ways, shape):
    rows = sources[0].shape[0]

    def body(place_ref, *refs):
        for way in range(ways):
            for part, (source, turn) in enumerate(parts):
                lanes = head_lane(place_ref, way, 1, turn, shape)
                refs[-1][way, part] = refs[source][:, lanes]

    out = jax.ShapeDtypeStruct((ways, len(parts), rows, HEAD_DIM), sources[0].dtype)
    return in_vmem(body, out, "pack_twin", place, *sources)


def pack(place, sources, twin, messages, ways, shape):
    cores, _ = shape
    rows = sources[0].shape[0]
    operands = [*sources] + ([twin] if cores > 1 else [])

    def body(place_ref, *refs):
        ins, outs = refs[: len(operands)], refs[len(operands) :]
        offset = 0
        for at, parts in enumerate(messages):
            for way in range(ways):
                for part, (source, turn) in enumerate(parts):
                    lanes = head_lane(place_ref, way, 0, turn, shape)
                    outs[at * ways + way][0, part] = ins[source][:, lanes]
                    if cores > 1:
                        outs[at * ways + way][1, part] = ins[-1][way, offset + part]
            offset += len(parts)

    out = [
        jax.ShapeDtypeStruct((cores, len(parts), rows, HEAD_DIM), sources[0].dtype)
        for parts in messages
        for _ in range(ways)
    ]
    packed = in_vmem(body, out, "pack", place, *operands)
    return [packed[at * ways : (at + 1) * ways] for at in range(len(messages))]


def unpack(place, pieces, twins, shape):
    cores, turns = shape
    ways, rows = len(pieces[0]), pieces[0][0].shape[2]
    flat = [piece for group in pieces for piece in group]
    operands = flat + (twins if cores > 1 else [])

    def body(place_ref, *refs):
        for turn in range(turns):
            for way in range(ways):
                lanes = head_lane(place_ref, way, 0, turn, shape)
                refs[-1][:, lanes] = refs[turn * ways + way][0, 0]
                if cores > 1:
                    lanes = head_lane(place_ref, way, 1, turn, shape)
                    refs[-1][:, lanes] = refs[len(flat) + turn][way]

    out = jax.ShapeDtypeStruct((rows, ways * cores * turns * HEAD_DIM), flat[0].dtype)
    return in_vmem(body, out, "unpack", place, *operands)


def attend(place, layout, query_ids, key_ids, block_mask, turn, queries, parts, extra, shape):
    cores, turns = shape
    ways, rows = len(queries), queries[0].shape[2]
    query_part = queries[0].shape[1] - 1
    units = ways * cores * rows // BLOCK
    blocks = sum(part.shape[0] * part.shape[1] for part in parts) * cores * rows // BLOCK
    width = blocks * BLOCK
    group = max(1, min(units, SCORE_BYTES // (4 * BLOCK * width)))
    while units % group:
        group -= 1
    lots = []
    for which, part in enumerate(parts):
        held = part.shape[1] * cores * rows // BLOCK
        for member in range(part.shape[0]):
            lots += [
                (which, member, first, min(4, held - first)) for first in range(0, held, 4)
            ]

    def body(place_ref, layout_ref, query_ids_ref, key_ids_ref, mask_ref, *refs):
        query_refs, part_refs = refs[:ways], refs[ways : ways + len(parts)]
        extra_refs, out_refs = refs[ways + len(parts) : -3 - ways], refs[-3 - ways : -3]
        scores, asked, answered = refs[-3:]
        for way in range(ways):
            for other in range(cores):
                at = (way * cores + other) * rows
                asked[at : at + rows] = query_refs[way][other, query_part]

        def some(which, part, member, first, count):
            whole = part_refs[part][member, :, :, which].reshape(-1, HEAD_DIM)
            return whole[first * BLOCK : (first + count) * BLOCK]

        def step(lot, carry):
            tile = asked[pl.ds(pl.multiple_of(lot * group * BLOCK, BLOCK), group * BLOCK)]
            mask_rows = [layout_ref[query_ids_ref[lot * group + at]] for at in range(group)]
            maxima = [None] * group
            block = 0
            for lot_at in lots:
                found = lax.dot_general(
                    tile,
                    some(0, *lot_at),
                    (((1,), (1,)), ((), ())),
                    preferred_element_type=jnp.float32,
                )
                for unit in range(lot_at[-1]):
                    column = layout_ref[key_ids_ref[block]]
                    for at in range(group):
                        allowed = mask_ref[0, mask_rows[at], column] > 0
                        bias = jnp.where(allowed, jnp.float32(0), jnp.float32(-jnp.inf))
                        piece = (
                            found[
                                at * BLOCK : (at + 1) * BLOCK, unit * BLOCK : (unit + 1) * BLOCK
                            ]
                            + bias
                        )
                        scores[
                            at * BLOCK : (at + 1) * BLOCK, block * BLOCK : (block + 1) * BLOCK
                        ] = piece
                        maxima[at] = piece if maxima[at] is None else jnp.maximum(maxima[at], piece)
                    block += 1
            for at in range(group):
                shift = jnp.max(maxima[at], axis=1, keepdims=True) * EXP2_SCALE
                total = accum = None
                block = 0
                for lot_at in lots:
                    count = lot_at[-1]
                    wide = scores[
                        at * BLOCK : (at + 1) * BLOCK, block * BLOCK : (block + count) * BLOCK
                    ]
                    probs = jnp.exp2(wide * EXP2_SCALE - shift)
                    for unit in range(count):
                        piece = probs[:, unit * BLOCK : (unit + 1) * BLOCK]
                        total = piece if total is None else total + piece
                    product = jnp.dot(
                        probs.astype(jnp.bfloat16),
                        some(1, *lot_at),
                        preferred_element_type=jnp.float32,
                    )
                    accum = product if accum is None else accum + product
                    block += count
                total = jnp.sum(total, axis=1, keepdims=True)
                spot = pl.multiple_of((lot * group + at) * BLOCK, BLOCK)
                answered[pl.ds(spot, BLOCK)] = (accum / total).astype(jnp.bfloat16)
            return carry

        lax.fori_loop(0, units // group, step, 0)
        for way in range(ways):
            for other in range(cores):
                at = (way * cores + other) * rows
                out_refs[way][other, 0] = answered[at : at + rows]
                if extra:
                    out_refs[way][other, 1] = extra_refs[way][other, 0]

    whole = pl.BlockSpec(memory_space=pltpu.VMEM)
    return pl.pallas_call(
        body,
        grid_spec=pltpu.PrefetchScalarGridSpec(
            num_scalar_prefetch=4,
            grid=(1,),
            in_specs=[
                pl.BlockSpec(
                    (1, blocks, blocks),
                    lambda step, place, *_: (place[0] * turns + turn, 0, 0),
                    memory_space=pltpu.SMEM,
                )
            ]
            + [whole] * (ways + len(parts) + len(extra)),
            out_specs=[whole] * ways,
            scratch_shapes=[
                pltpu.VMEM((group * BLOCK, width), jnp.float32),
                pltpu.VMEM((units * BLOCK, HEAD_DIM), jnp.bfloat16),
                pltpu.VMEM((units * BLOCK, HEAD_DIM), jnp.bfloat16),
            ],
        ),
        out_shape=[
            jax.ShapeDtypeStruct((cores, 2 if extra else 1, rows, HEAD_DIM), jnp.bfloat16)
        ]
        * ways,
        compiler_params=pltpu.CompilerParams(vmem_limit_bytes=KERNEL_VMEM),
        cost_estimate=pl.CostEstimate(
            flops=40 * units * BLOCK * width * HEAD_DIM,
            bytes_accessed=4 * width * HEAD_DIM,
            transcendentals=units * BLOCK * width,
        ),
        name="attend",
    )(place, layout, query_ids, key_ids, block_mask, *queries, *parts, *extra)


def after(array, *others):
    return lax.optimization_barrier((array, *others))[0]


def per_device(queries, key_vectors, value_vectors, block_mask, layout):
    ways, seq_count = lax.axis_size("head"), lax.axis_size("seq")
    seq, way_here = lax.axis_index("seq"), lax.axis_index("head")
    rows, width = queries.shape
    heads_here = width // HEAD_DIM // ways
    relay = seq_count == 8 and heads_here % 2 == 0
    cores = 2 if relay else 1
    turns = heads_here // cores
    shape = (cores, turns)
    assert BLOCK % rows == 0 and ways & (ways - 1) == 0 and ways * rows % BLOCK == 0
    fold = BLOCK // rows
    assert fold == 1 or cores == 1
    chip, core = seq // cores, seq % cores
    place = jnp.stack([core, way_here]).astype(jnp.int32)
    near = [(s, s ^ (4 if s & 1 else 2)) for s in range(8)]
    far = [(s, s ^ (2 if s & 1 else 4)) for s in range(8)]
    twins = [(s, s ^ 1) for s in range(8)]
    if relay:
        flip = 1 + core
        chips = jnp.stack([chip, chip ^ flip, chip ^ 3 ^ flip, chip ^ 3])
    else:
        chips = jnp.arange(seq_count)

    def block_ids(of_chips):
        of_core = of_chips[:, None, None] * cores + (core ^ jnp.arange(cores))[None, None, :]
        of_way = (way_here ^ jnp.arange(0, ways, fold))[None, :, None]
        return ((of_core * ways + of_way) // fold).reshape(-1).astype(jnp.int32)

    query_ids, key_ids = block_ids(chip[None]), block_ids(chips)

    def swap(array, way):
        return lax.ppermute(array, "head", [(z, z ^ way) for z in range(ways)])

    def send(array, pairs):
        return lax.ppermute(array, "seq", pairs)

    sources = (key_vectors, value_vectors, queries)
    messages = [
        [(0, turn), (1, turn)] + ([(2, turn - 1)] if turn else []) for turn in range(turns)
    ]
    messages.append([(2, turns - 1)])
    rest = [part for parts in messages[1:] for part in parts]
    if relay:
        first_twin = send(pack_twin(place, sources[:2], messages[0], ways, shape), twins)
        sent = pack(place, sources[:2], first_twin, messages[:1], ways, shape)
        rest_twin = pack_twin(place, sources, rest, ways, shape)
        rest_twin = send(after(rest_twin, sent[0][0]), twins)
    else:
        sent, rest_twin = pack(place, sources[:2], None, messages[:1], ways, shape), None
    sent += pack(place, sources, rest_twin, messages[1:], ways, shape)

    held, shared, pieces, outs, returned, back = [], [], [], [], [], []

    def exchange(turn):
        got = [sent[turn][0]]
        for way in range(1, ways):
            message = sent[turn][way]
            if turn:
                message = after(message, held[turn - 1][way])
            if turn > 1:
                message = after(message, *pieces[turn - 2][-2:])
            got.append(swap(message, way))
        held.append(got)

    def gather(turn):
        got = list(held[turn])
        earlier = pieces[turn - 1][-2:] if turn else [sent[1][0]]
        got[0] = after(got[0], *earlier)
        joined = jnp.stack([piece[:, :2] for piece in got], axis=0)
        shared.append(joined)
        if not relay:
            return [lax.all_gather(joined, "seq", axis=0)]
        first, second = send(joined, near), send(joined, far)
        half = ways // 2
        parts = [joined, first, second]

        def onward(outs):
            waits = list(outs) + (returned[0] if turn == turns - 1 else [])
            one, two = lax.optimization_barrier((first[:half], second[half:], *waits))[:2]
            if turn == turns - 1:
                sidelong.extend([one, two])
            return [part[None] for part in parts + [send(one, far), send(two, near)]]

        return onward

    def bring_back(turn):
        result = outs[turn]
        if turn + 2 < turns:
            result = lax.optimization_barrier((*result, shared[turn + 2]))[:-1]
        elif turn + 1 < turns:
            result = lax.optimization_barrier((*result, *sidelong))[: len(result)]
        result = [result[0]] + [swap(result[way], way) for way in range(1, ways)]
        returned.append(result)
        if relay:
            back.append(send(jnp.stack([piece[1, 0] for piece in result]), twins))

    sidelong = []
    exchange(0)
    pieces.append(gather(0))
    if relay:
        pieces[0] = pieces[0]([])
    exchange(1)
    for turn in range(turns):
        if turn + 2 < turns:
            exchange(turn + 2)
        parts = list(pieces[turn])
        onward = None
        if turn + 1 < turns:
            onward = gather(turn + 1)
            parts[0] = after(parts[0], shared[turn + 1])
        asked = held[turn + 1] if turn + 1 < turns else returned[0]
        extra = sent[turns] if turn == 0 else []
        outs.append(
            attend(
                place, layout, query_ids, key_ids, block_mask, turn, asked, parts, extra, shape
            )
        )
        if turn and turn + 1 < turns:
            bring_back(turn - 1)
        if turn + 1 < turns:
            pieces.append(onward(outs[turn]) if relay else onward)
    for turn in range(len(returned), turns):
        bring_back(turn)
    return unpack(place, returned, back, shape)


def solution(mesh):
    placed = (
        P(("seq", "head"), None),
        P(("seq", "head"), None),
        P(("seq", "head"), None),
        P("head", None, None),
        P(),
    )
    return jax.shard_map(
        per_device, mesh=mesh, in_specs=placed, out_specs=P(("seq", "head"), None), check_vma=False
    )
```

```python
import math

import jax
import jax.numpy as jnp
from jax import lax
from jax.experimental import pallas as pl
from jax.experimental.pallas import tpu as pltpu
from jax.sharding import PartitionSpec as P

HEAD_DIM = 128
BLOCK = 128
EXP2_SCALE = math.log2(math.e) / math.sqrt(HEAD_DIM)
KERNEL_VMEM = 32 * 2**20
SCORE_BYTES = 8 * 2**20


def head_lane(place_ref, way, other, turn, shape):
    cores, turns = shape
    core = place_ref[0] ^ other if cores > 1 else 0
    head = ((place_ref[1] ^ way) * cores + core) * turns + turn
    return pl.ds(pl.multiple_of(head * HEAD_DIM, HEAD_DIM), HEAD_DIM)


def in_vmem(body, out_shape, name, place, *operands):
    return pl.pallas_call(
        body,
        in_specs=[pl.BlockSpec(memory_space=pltpu.SMEM)]
        + [pl.BlockSpec(memory_space=pltpu.VMEM)] * len(operands),
        out_specs=jax.tree.map(lambda _: pl.BlockSpec(memory_space=pltpu.VMEM), out_shape),
        out_shape=out_shape,
        name=name,
    )(place, *operands)


def pack_twin(place, sources, parts, ways, shape):
    rows = sources[0].shape[0]

    def body(place_ref, *refs):
        for way in range(ways):
            for part, (source, turn) in enumerate(parts):
                lanes = head_lane(place_ref, way, 1, turn, shape)
                refs[-1][way, part] = refs[source][:, lanes]

    out = jax.ShapeDtypeStruct((ways, len(parts), rows, HEAD_DIM), sources[0].dtype)
    return in_vmem(body, out, "pack_twin", place, *sources)


def pack(place, sources, twin, messages, ways, shape):
    cores, _ = shape
    rows = sources[0].shape[0]
    operands = [*sources] + ([twin] if cores > 1 else [])

    def body(place_ref, *refs):
        ins, outs = refs[: len(operands)], refs[len(operands) :]
        offset = 0
        for at, parts in enumerate(messages):
            for way in range(ways):
                for part, (source, turn) in enumerate(parts):
                    lanes = head_lane(place_ref, way, 0, turn, shape)
                    outs[at * ways + way][0, part] = ins[source][:, lanes]
                    if cores > 1:
                        outs[at * ways + way][1, part] = ins[-1][way, offset + part]
            offset += len(parts)

    out = [
        jax.ShapeDtypeStruct((cores, len(parts), rows, HEAD_DIM), sources[0].dtype)
        for parts in messages
        for _ in range(ways)
    ]
    packed = in_vmem(body, out, "pack", place, *operands)
    return [packed[at * ways : (at + 1) * ways] for at in range(len(messages))]


def unpack(place, pieces, twins, shape):
    cores, turns = shape
    ways, rows = len(pieces[0]), pieces[0][0].shape[2]
    flat = [piece for group in pieces for piece in group]
    operands = flat + (twins if cores > 1 else [])

    def body(place_ref, *refs):
        for turn in range(turns):
            for way in range(ways):
                lanes = head_lane(place_ref, way, 0, turn, shape)
                refs[-1][:, lanes] = refs[turn * ways + way][0, 0]
                if cores > 1:
                    lanes = head_lane(place_ref, way, 1, turn, shape)
                    refs[-1][:, lanes] = refs[len(flat) + turn][way]

    out = jax.ShapeDtypeStruct((rows, ways * cores * turns * HEAD_DIM), flat[0].dtype)
    return in_vmem(body, out, "unpack", place, *operands)


def attend(
    place, layout, query_ids, key_ids, block_mask, turn, queries, parts, extra, shape, state, first_block, last
):
    cores, turns = shape
    ways, rows = len(queries), queries[0].shape[2]
    query_part = queries[0].shape[1] - 1
    units = ways * cores * rows // BLOCK
    blocks = sum(part.shape[0] * part.shape[1] for part in parts) * cores * rows // BLOCK
    mask_blocks = layout.shape[0]
    width = blocks * BLOCK
    group = max(1, min(units, SCORE_BYTES // (4 * BLOCK * width)))
    while units % group:
        group -= 1
    lots = []
    for which, part in enumerate(parts):
        held = part.shape[1] * cores * rows // BLOCK
        for member in range(part.shape[0]):
            lots += [
                (which, member, first, min(4, held - first)) for first in range(0, held, 4)
            ]

    def body(place_ref, layout_ref, query_ids_ref, key_ids_ref, mask_ref, *refs):
        query_refs, part_refs = refs[:ways], refs[ways : ways + len(parts)]
        state_refs = refs[ways + len(parts) :][: len(state)]
        extra_refs = refs[ways + len(parts) + len(state) :][: len(extra)]
        out_refs = refs[ways + len(parts) + len(state) + len(extra) : -3]
        scores, asked, answered = refs[-3:]
        for way in range(ways):
            for other in range(cores):
                at = (way * cores + other) * rows
                asked[at : at + rows] = query_refs[way][other, query_part]

        def some(which, part, member, first, count):
            whole = part_refs[part][member, :, :, which].reshape(-1, HEAD_DIM)
            return whole[first * BLOCK : (first + count) * BLOCK]

        def step(lot, carry):
            tile = asked[pl.ds(pl.multiple_of(lot * group * BLOCK, BLOCK), group * BLOCK)]
            mask_rows = [layout_ref[query_ids_ref[lot * group + at]] for at in range(group)]
            spots = [
                pl.ds(pl.multiple_of((lot * group + at) * BLOCK, BLOCK), BLOCK) for at in range(group)
            ]
            maxima = [state_refs[0][spot] if state else None for spot in spots]
            block = 0
            for lot_at in lots:
                found = lax.dot_general(
                    tile,
                    some(0, *lot_at),
                    (((1,), (1,)), ((), ())),
                    preferred_element_type=jnp.float32,
                )
                for unit in range(lot_at[-1]):
                    column = layout_ref[key_ids_ref[first_block + block]]
                    for at in range(group):
                        allowed = mask_ref[0, mask_rows[at], column] > 0
                        bias = jnp.where(allowed, jnp.float32(0), jnp.float32(-jnp.inf))
                        piece = (
                            found[
                                at * BLOCK : (at + 1) * BLOCK, unit * BLOCK : (unit + 1) * BLOCK
                            ]
                            + bias
                        )
                        scores[
                            at * BLOCK : (at + 1) * BLOCK, block * BLOCK : (block + 1) * BLOCK
                        ] = piece
                        maxima[at] = piece if maxima[at] is None else jnp.maximum(maxima[at], piece)
                    block += 1
            for at in range(group):
                peak = jnp.max(maxima[at], axis=1, keepdims=True)
                shift = peak * EXP2_SCALE
                total = accum = None
                if state:
                    factor = jnp.exp2(state_refs[0][spots[at]] * EXP2_SCALE - shift)
                    total = state_refs[1][spots[at]] * factor
                    accum = state_refs[2][spots[at]] * factor
                block = 0
                for lot_at in lots:
                    count = lot_at[-1]
                    wide = scores[
                        at * BLOCK : (at + 1) * BLOCK, block * BLOCK : (block + count) * BLOCK
                    ]
                    probs = jnp.exp2(wide * EXP2_SCALE - shift)
                    for unit in range(count):
                        piece = probs[:, unit * BLOCK : (unit + 1) * BLOCK]
                        total = piece if total is None else total + piece
                    product = jnp.dot(
                        probs.astype(jnp.bfloat16),
                        some(1, *lot_at),
                        preferred_element_type=jnp.float32,
                    )
                    accum = product if accum is None else accum + product
                    block += count
                if last:
                    total = jnp.sum(total, axis=1, keepdims=True)
                    answered[spots[at]] = (accum / total).astype(jnp.bfloat16)
                else:
                    out_refs[0][spots[at]] = jnp.broadcast_to(peak, (BLOCK, HEAD_DIM))
                    out_refs[1][spots[at]] = total
                    out_refs[2][spots[at]] = accum
            return carry

        lax.fori_loop(0, units // group, step, 0)
        for way in range(ways if last else 0):
            for other in range(cores):
                at = (way * cores + other) * rows
                out_refs[way][other, 0] = answered[at : at + rows]
                if extra:
                    out_refs[way][other, 1] = extra_refs[way][other, 0]

    if last:
        out_shape = [
            jax.ShapeDtypeStruct((cores, 2 if extra else 1, rows, HEAD_DIM), jnp.bfloat16)
        ] * ways
    else:
        out_shape = [jax.ShapeDtypeStruct((units * BLOCK, HEAD_DIM), jnp.float32)] * 3
    whole = pl.BlockSpec(memory_space=pltpu.VMEM)
    return pl.pallas_call(
        body,
        grid_spec=pltpu.PrefetchScalarGridSpec(
            num_scalar_prefetch=4,
            grid=(1,),
            in_specs=[
                pl.BlockSpec(
                    (1, mask_blocks, mask_blocks),
                    lambda step, place, *_: (place[0] * turns + turn, 0, 0),
                    memory_space=pltpu.SMEM,
                )
            ]
            + [whole] * (ways + len(parts) + len(state) + len(extra)),
            out_specs=[whole] * len(out_shape),
            scratch_shapes=[
                pltpu.VMEM((group * BLOCK, width), jnp.float32),
                pltpu.VMEM((units * BLOCK, HEAD_DIM), jnp.bfloat16),
                pltpu.VMEM((units * BLOCK, HEAD_DIM), jnp.bfloat16),
            ],
        ),
        out_shape=out_shape,
        compiler_params=pltpu.CompilerParams(vmem_limit_bytes=KERNEL_VMEM),
        cost_estimate=pl.CostEstimate(
            flops=40 * units * BLOCK * width * HEAD_DIM,
            bytes_accessed=4 * width * HEAD_DIM,
            transcendentals=units * BLOCK * width,
        ),
        name="attend",
    )(place, layout, query_ids, key_ids, block_mask, *queries, *parts, *state, *extra)


def after(array, *others):
    return lax.optimization_barrier((array, *others))[0]


def per_device(queries, key_vectors, value_vectors, block_mask, layout):
    ways, seq_count = lax.axis_size("head"), lax.axis_size("seq")
    seq, way_here = lax.axis_index("seq"), lax.axis_index("head")
    rows, width = queries.shape
    heads_here = width // HEAD_DIM // ways
    relay = seq_count == 8 and heads_here % 2 == 0
    cores = 2 if relay else 1
    turns = heads_here // cores
    shape = (cores, turns)
    assert BLOCK % rows == 0 and ways & (ways - 1) == 0 and ways * rows % BLOCK == 0
    fold = BLOCK // rows
    assert fold == 1 or cores == 1
    chip, core = seq // cores, seq % cores
    place = jnp.stack([core, way_here]).astype(jnp.int32)
    near = [(s, s ^ (4 if s & 1 else 2)) for s in range(8)]
    far = [(s, s ^ (2 if s & 1 else 4)) for s in range(8)]
    twins = [(s, s ^ 1) for s in range(8)]
    if relay:
        flip = 1 + core
        chips = jnp.stack([chip, chip ^ flip, chip ^ 3 ^ flip, chip ^ 3])
    else:
        chips = jnp.arange(seq_count)

    def block_ids(of_chips):
        of_core = of_chips[:, None, None] * cores + (core ^ jnp.arange(cores))[None, None, :]
        of_way = (way_here ^ jnp.arange(0, ways, fold))[None, :, None]
        return ((of_core * ways + of_way) // fold).reshape(-1).astype(jnp.int32)

    query_ids, key_ids = block_ids(chip[None]), block_ids(chips)

    def swap(array, way):
        return lax.ppermute(array, "head", [(z, z ^ way) for z in range(ways)])

    def send(array, pairs):
        return lax.ppermute(array, "seq", pairs)

    sources = (key_vectors, value_vectors, queries)
    messages = [
        [(0, turn), (1, turn)] + ([(2, turn - 1)] if turn else []) for turn in range(turns)
    ]
    messages.append([(2, turns - 1)])
    rest = [part for parts in messages[1:] for part in parts]
    if relay:
        first_twin = send(pack_twin(place, sources[:2], messages[0], ways, shape), twins)
        sent = pack(place, sources[:2], first_twin, messages[:1], ways, shape)
        rest_twin = pack_twin(place, sources, rest, ways, shape)
        rest_twin = send(after(rest_twin, sent[0][0]), twins)
    else:
        sent, rest_twin = pack(place, sources[:2], None, messages[:1], ways, shape), None
    sent += pack(place, sources, rest_twin, messages[1:], ways, shape)

    held, shared, pieces, outs, returned, back = [], [], [], [], [], []

    def exchange(turn):
        got = [sent[turn][0]]
        for way in range(1, ways):
            message = sent[turn][way]
            if turn:
                message = after(message, held[turn - 1][way])
            if turn > 1:
                message = after(message, *pieces[turn - 2][-2:])
            got.append(swap(message, way))
        held.append(got)

    def gather(turn):
        got = list(held[turn])
        earlier = pieces[turn - 1][-2:] if turn else [sent[1][0]]
        got[0] = after(got[0], *earlier)
        joined = jnp.stack([piece[:, :2] for piece in got], axis=0)
        shared.append(joined)
        if not relay:
            return [lax.all_gather(joined, "seq", axis=0)]
        first, second = send(joined, near), send(joined, far)
        half = ways // 2
        parts = [joined, first, second]

        def onward(outs):
            waits = list(outs) + (returned[0] if turn == turns - 1 else [])
            one, two = lax.optimization_barrier((first[:half], second[half:], *waits))[:2]
            if turn == turns - 1:
                sidelong.extend([one, two])
            return [part[None] for part in parts + [send(one, far), send(two, near)]]

        return onward

    def bring_back(turn):
        result = outs[turn]
        if turn + 2 < turns:
            result = lax.optimization_barrier((*result, shared[turn + 2]))[:-1]
        elif turn + 1 < turns:
            result = lax.optimization_barrier((*result, *sidelong))[: len(result)]
        result = [result[0]] + [swap(result[way], way) for way in range(1, ways)]
        returned.append(result)

    sidelong = []
    exchange(0)
    pieces.append(gather(0))
    if relay:
        pieces[0] = pieces[0]([])
    exchange(1)
    for turn in range(turns):
        if turn + 2 < turns:
            exchange(turn + 2)
        parts = list(pieces[turn])
        onward = None
        if turn + 1 < turns:
            onward = gather(turn + 1)
            parts[0] = after(parts[0], shared[turn + 1])
        asked = held[turn + 1] if turn + 1 < turns else returned[0]
        extra = sent[turns] if turn == 0 else []
        fixed = (place, layout, query_ids, key_ids, block_mask, turn, asked)
        state, first_block = [], 0
        if relay and turn + 1 == turns:
            state = attend(*fixed, parts[:3], [], shape, [], 0, False)
            first_block, parts = 3 * ways * cores, parts[3:]
        outs.append(attend(*fixed, parts, extra, shape, state, first_block, True))
        if turn and turn + 1 < turns:
            bring_back(turn - 1)
        if turn + 1 < turns:
            pieces.append(onward(outs[turn]) if relay else onward)
    for turn in range(len(returned), turns):
        bring_back(turn)
    for result in returned if relay else []:
        joined = jnp.stack([piece[1, 0] for piece in result])
        back.append(send(after(joined, outs[-1][0]), twins))
    return unpack(place, returned, back, shape)


def solution(mesh):
    placed = (
        P(("seq", "head"), None),
        P(("seq", "head"), None),
        P(("seq", "head"), None),
        P("head", None, None),
        P(),
    )
    return jax.shard_map(
        per_device, mesh=mesh, in_specs=placed, out_specs=P(("seq", "head"), None), check_vma=False
    )
```

```python
import math

import jax
import jax.numpy as jnp
from jax import lax
from jax.experimental import pallas as pl
from jax.experimental.pallas import tpu as pltpu
from jax.sharding import PartitionSpec as P

HEAD_DIM = 128
BLOCK = 128
EXP2_SCALE = math.log2(math.e) / math.sqrt(HEAD_DIM)
KERNEL_VMEM = 40 * 2**20
SCORE_BYTES = 16 * 2**20


def head_lane(place_ref, way, other, turn, shape):
    cores, turns = shape
    core = place_ref[0] ^ other if cores > 1 else 0
    head = ((place_ref[1] ^ way) * cores + core) * turns + turn
    return pl.ds(pl.multiple_of(head * HEAD_DIM, HEAD_DIM), HEAD_DIM)


def in_vmem(body, out_shape, name, place, *operands):
    return pl.pallas_call(
        body,
        in_specs=[pl.BlockSpec(memory_space=pltpu.SMEM)]
        + [pl.BlockSpec(memory_space=pltpu.VMEM)] * len(operands),
        out_specs=jax.tree.map(lambda _: pl.BlockSpec(memory_space=pltpu.VMEM), out_shape),
        out_shape=out_shape,
        name=name,
    )(place, *operands)


def pack_twin(place, sources, parts, ways, shape):
    rows = sources[0].shape[0]

    def body(place_ref, *refs):
        for way in range(ways):
            for part, (source, turn) in enumerate(parts):
                lanes = head_lane(place_ref, way, 1, turn, shape)
                refs[-1][way, part] = refs[source][:, lanes]

    out = jax.ShapeDtypeStruct((ways, len(parts), rows, HEAD_DIM), sources[0].dtype)
    return in_vmem(body, out, "pack_twin", place, *sources)


def pack(place, sources, twin, messages, ways, shape):
    cores, _ = shape
    rows = sources[0].shape[0]
    operands = [*sources] + ([twin] if cores > 1 else [])

    def body(place_ref, *refs):
        ins, outs = refs[: len(operands)], refs[len(operands) :]
        offset = 0
        for at, parts in enumerate(messages):
            for way in range(ways):
                for part, (source, turn) in enumerate(parts):
                    lanes = head_lane(place_ref, way, 0, turn, shape)
                    outs[at * ways + way][0, part] = ins[source][:, lanes]
                    if cores > 1:
                        outs[at * ways + way][1, part] = ins[-1][way, offset + part]
            offset += len(parts)

    out = [
        jax.ShapeDtypeStruct((cores, len(parts), rows, HEAD_DIM), sources[0].dtype)
        for parts in messages
        for _ in range(ways)
    ]
    packed = in_vmem(body, out, "pack", place, *operands)
    return [packed[at * ways : (at + 1) * ways] for at in range(len(messages))]


def unpack(place, pieces, twins, shape):
    cores, turns = shape
    ways, rows = len(pieces[0]), pieces[0][0].shape[2]
    flat = [piece for group in pieces for piece in group]
    operands = flat + (twins if cores > 1 else [])

    def body(place_ref, *refs):
        for turn in range(turns):
            for way in range(ways):
                lanes = head_lane(place_ref, way, 0, turn, shape)
                refs[-1][:, lanes] = refs[turn * ways + way][0, 0]
                if cores > 1:
                    lanes = head_lane(place_ref, way, 1, turn, shape)
                    refs[-1][:, lanes] = refs[len(flat) + turn][way]

    out = jax.ShapeDtypeStruct((rows, ways * cores * turns * HEAD_DIM), flat[0].dtype)
    return in_vmem(body, out, "unpack", place, *operands)


def attend(
    place, layout, query_ids, key_ids, block_mask, turn, queries, parts, extra, shape, state, first_block, last
):
    cores, turns = shape
    ways, rows = len(queries), queries[0].shape[2]
    query_part = queries[0].shape[1] - 1
    units = ways * cores * rows // BLOCK
    blocks = sum(part.shape[0] * part.shape[1] for part in parts) * cores * rows // BLOCK
    mask_blocks = layout.shape[0]
    width = blocks * BLOCK
    group = max(1, min(units, SCORE_BYTES // (4 * BLOCK * width)))
    while units % group:
        group -= 1
    lots = []
    for which, part in enumerate(parts):
        held = part.shape[1] * cores * rows // BLOCK
        for member in range(part.shape[0]):
            lots += [
                (which, member, first, min(4, held - first)) for first in range(0, held, 4)
            ]

    def body(place_ref, layout_ref, query_ids_ref, key_ids_ref, mask_ref, *refs):
        query_refs, part_refs = refs[:ways], refs[ways : ways + len(parts)]
        state_refs = refs[ways + len(parts) :][: len(state)]
        extra_refs = refs[ways + len(parts) + len(state) :][: len(extra)]
        out_refs = refs[ways + len(parts) + len(state) + len(extra) : -3]
        scores, asked, answered = refs[-3:]
        for way in range(ways):
            for other in range(cores):
                at = (way * cores + other) * rows
                asked[at : at + rows] = query_refs[way][other, query_part]

        def some(which, part, member, first, count):
            whole = part_refs[part][member, :, :, which].reshape(-1, HEAD_DIM)
            return whole[first * BLOCK : (first + count) * BLOCK]

        def step(lot, carry):
            tile = asked[pl.ds(pl.multiple_of(lot * group * BLOCK, BLOCK), group * BLOCK)]
            mask_rows = [layout_ref[query_ids_ref[lot * group + at]] for at in range(group)]
            spots = [
                pl.ds(pl.multiple_of((lot * group + at) * BLOCK, BLOCK), BLOCK) for at in range(group)
            ]
            maxima = [state_refs[0][spot] if state else None for spot in spots]
            block = 0
            for lot_at in lots:
                found = lax.dot_general(
                    tile,
                    some(0, *lot_at),
                    (((1,), (1,)), ((), ())),
                    preferred_element_type=jnp.float32,
                )
                for unit in range(lot_at[-1]):
                    column = layout_ref[key_ids_ref[first_block + block]]
                    for at in range(group):
                        allowed = mask_ref[0, mask_rows[at], column] > 0
                        bias = jnp.where(allowed, jnp.float32(0), jnp.float32(-jnp.inf))
                        piece = (
                            found[
                                at * BLOCK : (at + 1) * BLOCK, unit * BLOCK : (unit + 1) * BLOCK
                            ]
                            + bias
                        )
                        scores[
                            at * BLOCK : (at + 1) * BLOCK, block * BLOCK : (block + 1) * BLOCK
                        ] = piece
                        maxima[at] = piece if maxima[at] is None else jnp.maximum(maxima[at], piece)
                    block += 1
            for at in range(group):
                peak = jnp.max(maxima[at], axis=1, keepdims=True)
                shift = peak * EXP2_SCALE
                total = accum = None
                if state:
                    factor = jnp.exp2(state_refs[0][spots[at]] * EXP2_SCALE - shift)
                    total = state_refs[1][spots[at]] * factor
                    accum = state_refs[2][spots[at]] * factor
                block = 0
                for lot_at in lots:
                    count = lot_at[-1]
                    wide = scores[
                        at * BLOCK : (at + 1) * BLOCK, block * BLOCK : (block + count) * BLOCK
                    ]
                    probs = jnp.exp2(wide * EXP2_SCALE - shift)
                    for unit in range(count):
                        piece = probs[:, unit * BLOCK : (unit + 1) * BLOCK]
                        total = piece if total is None else total + piece
                    product = jnp.dot(
                        probs.astype(jnp.bfloat16),
                        some(1, *lot_at),
                        preferred_element_type=jnp.float32,
                    )
                    accum = product if accum is None else accum + product
                    block += count
                if last:
                    total = jnp.sum(total, axis=1, keepdims=True)
                    answered[spots[at]] = (accum / total).astype(jnp.bfloat16)
                else:
                    out_refs[0][spots[at]] = jnp.broadcast_to(peak, (BLOCK, HEAD_DIM))
                    out_refs[1][spots[at]] = total
                    out_refs[2][spots[at]] = accum
            return carry

        lax.fori_loop(0, units // group, step, 0)
        for way in range(ways if last else 0):
            for other in range(cores):
                at = (way * cores + other) * rows
                out_refs[way][other, 0] = answered[at : at + rows]
                if extra:
                    out_refs[way][other, 1] = extra_refs[way][other, 0]

    if last:
        out_shape = [
            jax.ShapeDtypeStruct((cores, 2 if extra else 1, rows, HEAD_DIM), jnp.bfloat16)
        ] * ways
    else:
        out_shape = [jax.ShapeDtypeStruct((units * BLOCK, HEAD_DIM), jnp.float32)] * 3
    whole = pl.BlockSpec(memory_space=pltpu.VMEM)
    return pl.pallas_call(
        body,
        grid_spec=pltpu.PrefetchScalarGridSpec(
            num_scalar_prefetch=4,
            grid=(1,),
            in_specs=[
                pl.BlockSpec(
                    (1, mask_blocks, mask_blocks),
                    lambda step, place, *_: (place[0] * turns + turn, 0, 0),
                    memory_space=pltpu.SMEM,
                )
            ]
            + [whole] * (ways + len(parts) + len(state) + len(extra)),
            out_specs=[whole] * len(out_shape),
            scratch_shapes=[
                pltpu.VMEM((group * BLOCK, width), jnp.float32),
                pltpu.VMEM((units * BLOCK, HEAD_DIM), jnp.bfloat16),
                pltpu.VMEM((units * BLOCK, HEAD_DIM), jnp.bfloat16),
            ],
        ),
        out_shape=out_shape,
        compiler_params=pltpu.CompilerParams(vmem_limit_bytes=KERNEL_VMEM),
        cost_estimate=pl.CostEstimate(
            flops=20 * units * BLOCK * width * HEAD_DIM,
            bytes_accessed=4 * width * HEAD_DIM,
            transcendentals=units * BLOCK * width,
        ),
        name="attend",
    )(place, layout, query_ids, key_ids, block_mask, *queries, *parts, *state, *extra)


def after(array, *others):
    return lax.optimization_barrier((array, *others))[0]


def per_device(queries, key_vectors, value_vectors, block_mask, layout):
    ways, seq_count = lax.axis_size("head"), lax.axis_size("seq")
    seq, way_here = lax.axis_index("seq"), lax.axis_index("head")
    rows, width = queries.shape
    heads_here = width // HEAD_DIM // ways
    relay = seq_count == 8 and heads_here % 2 == 0
    cores = 2 if relay else 1
    turns = heads_here // cores
    shape = (cores, turns)
    assert BLOCK % rows == 0 and ways & (ways - 1) == 0 and ways * rows % BLOCK == 0
    fold = BLOCK // rows
    assert fold == 1 or cores == 1
    chip, core = seq // cores, seq % cores
    place = jnp.stack([core, way_here]).astype(jnp.int32)
    near = [(s, s ^ (4 if s & 1 else 2)) for s in range(8)]
    far = [(s, s ^ (2 if s & 1 else 4)) for s in range(8)]
    twins = [(s, s ^ 1) for s in range(8)]
    if relay:
        flip = 1 + core
        chips = jnp.stack([chip, chip ^ flip, chip ^ 3 ^ flip, chip ^ 3])
    else:
        chips = jnp.arange(seq_count)

    def block_ids(of_chips):
        of_core = of_chips[:, None, None] * cores + (core ^ jnp.arange(cores))[None, None, :]
        of_way = (way_here ^ jnp.arange(0, ways, fold))[None, :, None]
        return ((of_core * ways + of_way) // fold).reshape(-1).astype(jnp.int32)

    query_ids, key_ids = block_ids(chip[None]), block_ids(chips)

    def swap(array, way):
        return lax.ppermute(array, "head", [(z, z ^ way) for z in range(ways)])

    def send(array, pairs):
        return lax.ppermute(array, "seq", pairs)

    sources = (key_vectors, value_vectors, queries)
    messages = [
        [(0, turn), (1, turn)] + ([(2, turn - 1)] if turn else []) for turn in range(turns)
    ]
    messages.append([(2, turns - 1)])
    rest = [part for parts in messages[1:] for part in parts]
    if relay:
        first_twin = send(pack_twin(place, sources[:2], messages[0], ways, shape), twins)
        sent = pack(place, sources[:2], first_twin, messages[:1], ways, shape)
        rest_twin = pack_twin(place, sources, rest, ways, shape)
        rest_twin = send(after(rest_twin, sent[0][0]), twins)
    else:
        sent, rest_twin = pack(place, sources[:2], None, messages[:1], ways, shape), None
    sent += pack(place, sources, rest_twin, messages[1:], ways, shape)

    held, shared, pieces, outs, returned, back = [], [], [], [], [], []

    def exchange(turn):
        got = [sent[turn][0]]
        for way in range(1, ways):
            message = sent[turn][way]
            if turn:
                message = after(message, held[turn - 1][way])
            if turn > 1:
                message = after(message, *pieces[turn - 2][-2:])
            got.append(swap(message, way))
        held.append(got)

    def gather(turn):
        got = list(held[turn])
        earlier = pieces[turn - 1][-2:] if turn else [sent[1][0]]
        got[0] = after(got[0], *earlier)
        joined = jnp.stack([piece[:, :2] for piece in got], axis=0)
        shared.append(joined)
        if not relay:
            return [lax.all_gather(joined, "seq", axis=0)]
        first, second = send(joined, near), send(joined, far)
        half = ways // 2
        parts = [joined, first, second]

        def onward(outs):
            waits = list(outs) + (returned[0] if turn == turns - 1 else [])
            one, two = lax.optimization_barrier((first[:half], second[half:], *waits))[:2]
            if turn == turns - 1:
                sidelong.extend([one, two])
            return [part[None] for part in parts + [send(one, far), send(two, near)]]

        return onward

    def bring_back(turn):
        result = outs[turn]
        if turn + 2 < turns:
            result = lax.optimization_barrier((*result, shared[turn + 2]))[:-1]
        elif turn + 1 < turns:
            result = lax.optimization_barrier((*result, *sidelong))[: len(result)]
        result = [result[0]] + [swap(result[way], way) for way in range(1, ways)]
        returned.append(result)

    sidelong = []
    exchange(0)
    pieces.append(gather(0))
    if relay:
        pieces[0] = pieces[0]([])
    exchange(1)
    for turn in range(turns):
        if turn + 2 < turns:
            exchange(turn + 2)
        parts = list(pieces[turn])
        onward = None
        if turn + 1 < turns:
            onward = gather(turn + 1)
            parts[0] = after(parts[0], shared[turn + 1])
        asked = held[turn + 1] if turn + 1 < turns else returned[0]
        extra = sent[turns] if turn == 0 else []
        fixed = (place, layout, query_ids, key_ids, block_mask, turn, asked)
        state, first_block = [], 0
        if relay and turn + 1 == turns:
            state = attend(*fixed, parts[:3], [], shape, [], 0, False)
            first_block, parts = 3 * ways * cores, parts[3:]
        outs.append(attend(*fixed, parts, extra, shape, state, first_block, True))
        if turn and turn + 1 < turns:
            bring_back(turn - 1)
        if turn + 1 < turns:
            pieces.append(onward(outs[turn]) if relay else onward)
    for turn in range(len(returned), turns):
        bring_back(turn)
    for result in returned if relay else []:
        joined = jnp.stack([piece[1, 0] for piece in result])
        back.append(send(after(joined, outs[-1][0]), twins))
    return unpack(place, returned, back, shape)


def solution(mesh):
    placed = (
        P(("seq", "head"), None),
        P(("seq", "head"), None),
        P(("seq", "head"), None),
        P("head", None, None),
        P(),
    )
    return jax.shard_map(
        per_device, mesh=mesh, in_specs=placed, out_specs=P(("seq", "head"), None), check_vma=False
    )
```
